512 devices in a mesh: ctx: 64 (over z_lo, x, core), grp: 8 (over z_hi, y).
Axes of the slice: x: 4, y: 4, z: 16 (z_hi: 2, z_lo: 8; z = z_hi * 8 + z_lo), core: 2. Of those that a mesh axis runs over, the one named last changes fastest.
Arguments:
- q_prompt: bfloat16 [4096, 64, 128], P('ctx', 'grp'), may hold values from -8 to 8
- k_prompt: bfloat16 [4096, 8, 128], P(('ctx', 'grp')), may hold values from -8 to 8
- v_prompt: bfloat16 [4096, 8, 128], P(('ctx', 'grp')), may hold values from -6 to 6
- grad_prompt: bfloat16 [4096, 64, 128], P('ctx', 'grp'), may hold values from -12 to 12
- q_roll: bfloat16 [4096, 64, 128], P('ctx', 'grp'), may hold values from -8 to 8
- k_roll: bfloat16 [4096, 8, 128], P('ctx', 'grp'), may hold values from -6 to 6
- v_roll: bfloat16 [4096, 8, 128], P('ctx', 'grp'), may hold values from -6 to 6
- grad_roll: bfloat16 [4096, 64, 128], P('ctx', 'grp'), may hold values from -12 to 12
- prompt_len: int32 [1], replicated, may hold values from 2049 to 4096
- roll_len: int32 [16], replicated, may hold values from 1 to 256, 3072 in all
Outputs:
- dq_prompt: bfloat16 [4096, 64, 128], P('ctx', 'grp')
- dk_prompt: bfloat16 [4096, 8, 128], P(('ctx', 'grp'))
- dv_prompt: bfloat16 [4096, 8, 128], P(('ctx', 'grp'))
- dq_roll: bfloat16 [4096, 64, 128], P('ctx', 'grp')
- dk_roll: bfloat16 [4096, 8, 128], P('ctx', 'grp')
- dv_roll: bfloat16 [4096, 8, 128], P('ctx', 'grp')
The draws below stay inside these ranges and needn't reach their ends.
Inputs may be any that keep to these rules, and one draw needn't show every extreme that they name: `roll_len`: some rollout has length 256.
All inputs are finite; a program needn't handle non-finite values.
Results may differ from the reference program's by a relative error of at most 0.0091.
Values may be sent and summed in bfloat16 or wider, within the bound.
No kernel may reach another device: no remote copies, remote signals or barrier semaphores. Data moves between devices by JAX's collectives and lax.ppermute only.
A program may use at most 64 MiB of HBM per device.

```python
import math
import jax
import jax.numpy as jnp
import numpy as np
from jax import lax

HEADS = 64
KVH = 8
HD = 128
RLEN = 256
PROMPT = 4096
ROLLOUTS = 16
ROLL_TOKENS = 4096


def draw_q_prompt(key, part):
    key = jax.random.fold_in(key, 11)
    values_drawn = jax.random.truncated_normal(key, -4.0, 4.0, (PROMPT, HEADS, HD), jnp.float32)
    return values_drawn.astype(jnp.bfloat16)


def draw_q_roll(key, part):
    key = jax.random.fold_in(key, 12)
    values_drawn = jax.random.truncated_normal(key, -4.0, 4.0, (ROLL_TOKENS, HEADS, HD), jnp.float32)
    return values_drawn.astype(jnp.bfloat16)


def draw_k_prompt(key, part):
    key = jax.random.fold_in(key, 13)
    values_drawn = jax.random.truncated_normal(key, -4.0, 4.0, (PROMPT, KVH, HD), jnp.float32)
    return values_drawn.astype(jnp.bfloat16)


def shard_levels(key, shape, split, low, top_value):
    loudness = 1.0
    for position, blocks in split:
        draws = jax.random.uniform(jax.random.fold_in(jax.random.fold_in(key, 6), position), (blocks,), jnp.float32, low / len(split), top_value / len(split))
        loudness = loudness * jnp.repeat(jnp.exp(draws), shape[position] // blocks).reshape((-1,) + (1,) * (len(shape) - 1 - position))
    return loudness


def profile(count, total, limit, lean):
    weights = [(1 << 20) // math.isqrt(standing ** lean) + 1 for standing in range(2, count + 1)]
    rest, given = total - limit - (count - 1), [1] * (count - 1)
    while rest > 0:
        candidates = [i for i in range(count - 1) if given[i] < limit]
        whole, left = sum([weights[i] for i in candidates]), rest
        for i in candidates:
            addition = min(limit - given[i], max(1, left * weights[i] // whole), rest)
            given[i] = given[i] + addition
            rest = rest - addition
    return np.array([limit] + given)


def uneven(stream_key, number_of, total, reach, skew):
    if number_of == 2:
        one = jax.random.randint(stream_key, (), max(1, total - reach), min(reach, total - 1) + 1)
        return jnp.stack([one, total - one])
    sizes = jnp.asarray(profile(number_of, total, reach, skew), jnp.int32)
    couples = (number_of - 1) // 2
    giver, receiver = sizes[1:1 + 2 * couples:2], sizes[2:2 + 2 * couples:2]
    margin = jnp.minimum(giver - 1, reach - receiver)
    shifted = jax.random.randint(jax.random.fold_in(stream_key, 1), (couples,), 0, 1 << 20) % (margin + 1)
    sizes = sizes.at[1:1 + 2 * couples:2].set(giver - shifted).at[2:2 + 2 * couples:2].set(receiver + shifted)
    return sizes[jax.random.permutation(jax.random.fold_in(stream_key, 2), number_of)]


def gaussian(stream_key, extent, width, reach, cuts=(), held_as=jnp.bfloat16):
    gain = shard_levels(stream_key, extent, cuts, -0.22, 0.18) if cuts else 1.0
    array = jax.random.normal(stream_key, extent, jnp.float32) * width * gain
    return jnp.minimum(jnp.maximum(array, -reach), reach).astype(held_as)


def setup_inputs(seed: int = 0) -> dict:
    streams_of = jax.random.split(jax.random.key(seed), 11)
    return {
        "q_prompt": draw_q_prompt(jax.random.fold_in(streams_of[10], 71), 0),
        "k_prompt": draw_k_prompt(jax.random.fold_in(streams_of[10], 71), 0),
        "v_prompt": gaussian(streams_of[2], (PROMPT, KVH, HD), 1.0, 6.0, ((0, 512),)),
        "grad_prompt": gaussian(streams_of[3], (PROMPT, HEADS, HD), 2.0, 12.0, ((0, 64), (1, 8))),
        "q_roll": draw_q_roll(jax.random.fold_in(streams_of[10], 71), 0),
        "k_roll": gaussian(streams_of[5], (ROLL_TOKENS, KVH, HD), 1.0, 6.0, ((0, 64), (1, 8))),
        "v_roll": gaussian(streams_of[6], (ROLL_TOKENS, KVH, HD), 1.0, 6.0, ((0, 64), (1, 8))),
        "grad_roll": gaussian(streams_of[7], (ROLL_TOKENS, HEADS, HD), 2.0, 12.0, ((0, 64), (1, 8))),
        "prompt_len": jax.random.randint(streams_of[8], (1,), PROMPT // 2 + 1, PROMPT + 1).astype(jnp.int32),
        "roll_len": uneven(streams_of[9], ROLLOUTS, ROLLOUTS * RLEN * 3 // 4, RLEN, 2).astype(jnp.int32),
    }


def attend(queries, out_grads, key_rows, value_rows, visible, scaling):
    query_f = queries.astype(jnp.float32)
    grad_f = out_grads.astype(jnp.float32)
    key_f = key_rows.astype(jnp.float32)
    value_f = value_rows.astype(jnp.float32)
    scores = jnp.einsum('rgd,kd->grk', query_f, key_f) * scaling
    scores = jnp.where(visible[None], scores, -jnp.inf)
    row_max = lax.optimization_barrier(jnp.max(scores, axis=-1, keepdims=True))
    row_sum = lax.optimization_barrier(jnp.sum(jnp.exp(scores - row_max), axis=-1, keepdims=True))
    log_total = row_max + jnp.log(row_sum)
    weights = jnp.exp(scores - log_total)
    rounded_weights = lax.optimization_barrier(weights.astype(jnp.bfloat16)).astype(jnp.float32)
    attended = jnp.einsum('grk,kd->grd', rounded_weights, value_f)
    delta_term = lax.optimization_barrier(jnp.sum(jnp.transpose(grad_f, (1, 0, 2)) * attended, axis=-1, keepdims=True))
    weight_grad = jnp.einsum('rgd,kd->grk', grad_f, value_f)
    score_grad = weights * (weight_grad - delta_term)
    rounded_grad = lax.optimization_barrier(score_grad.astype(jnp.bfloat16)).astype(jnp.float32)
    query_grad = jnp.einsum('grk,kd->rgd', rounded_grad, key_f) * scaling
    key_grad = jnp.einsum('grk,rgd->kd', rounded_grad, query_f) * scaling
    value_grad = jnp.einsum('grk,rgd->kd', rounded_weights, grad_f)
    return (query_grad, key_grad, value_grad)

def reference(q_prompt, k_prompt, v_prompt, grad_prompt, q_roll, k_roll, v_roll, grad_roll, prompt_len, roll_len):
    scaling = 1.0 / math.sqrt(HD)
    per_group = HEADS // KVH
    prompt_limit = prompt_len[0]
    prompt_pos = jnp.arange(PROMPT, dtype=jnp.int32)
    roll_pos = jnp.arange(RLEN, dtype=jnp.int32)
    q_roll = q_roll.reshape(ROLLOUTS, RLEN, HEADS, HD)
    k_roll = k_roll.reshape(ROLLOUTS, RLEN, KVH, HD)
    v_roll = v_roll.reshape(ROLLOUTS, RLEN, KVH, HD)
    grad_roll = grad_roll.reshape(ROLLOUTS, RLEN, HEADS, HD)
    prompt_keep = (prompt_pos < prompt_limit).astype(jnp.bfloat16)
    masked_prompt = grad_prompt * prompt_keep[:, None, None]
    roll_keep = (roll_pos[None, :] < roll_len[:, None]).astype(jnp.bfloat16)
    masked_roll = grad_roll * roll_keep[:, :, None, None]
    prompt_seen = (prompt_pos[None, :] <= prompt_pos[:, None]) & (prompt_pos[None, :] < prompt_limit)
    roll_seen = jnp.concatenate([jnp.broadcast_to(prompt_pos[None, :] < prompt_limit, (RLEN, PROMPT)), roll_pos[None, :] <= roll_pos[:, None]], axis=1)
    query_list, key_list, value_list = ([], [], [])
    roll_query_list, roll_key_list, roll_value_list = ([], [], [])
    for kv_head in range(KVH):
        first_head = kv_head * per_group
        last_head = first_head + per_group
        key_rows = k_prompt[:, kv_head]
        value_rows = v_prompt[:, kv_head]
        query_grad, key_grad, value_grad = attend(q_prompt[:, first_head:last_head], masked_prompt[:, first_head:last_head], key_rows, value_rows, prompt_seen, scaling)

        def per_rollout(summed, inputs):
            roll_queries, roll_grads, roll_keys, roll_values = inputs
            part_query, part_key, part_value = attend(roll_queries, roll_grads, jnp.concatenate([key_rows, roll_keys], axis=0), jnp.concatenate([value_rows, roll_values], axis=0), roll_seen, scaling)
            summed = (summed[0] + part_key[:PROMPT], summed[1] + part_value[:PROMPT])
            return (summed, (part_query.astype(jnp.bfloat16), part_key[PROMPT:].astype(jnp.bfloat16), part_value[PROMPT:].astype(jnp.bfloat16)))
        (key_total, value_total), (query_out, key_out, value_out) = lax.scan(per_rollout, (key_grad, value_grad), (q_roll[:, :, first_head:last_head], masked_roll[:, :, first_head:last_head], k_roll[:, :, kv_head], v_roll[:, :, kv_head]))
        query_list.append(query_grad.astype(jnp.bfloat16))
        key_list.append(key_total.astype(jnp.bfloat16))
        value_list.append(value_total.astype(jnp.bfloat16))
        roll_query_list.append(query_out)
        roll_key_list.append(key_out)
        roll_value_list.append(value_out)
    dq_prompt = jnp.concatenate(query_list, axis=1)
    dk_prompt = jnp.stack(key_list, axis=1)
    dv_prompt = jnp.stack(value_list, axis=1)
    dq_roll = jnp.concatenate(roll_query_list, axis=2).reshape(ROLL_TOKENS, HEADS, HD)
    dk_roll = jnp.stack(roll_key_list, axis=2).reshape(ROLL_TOKENS, KVH, HD)
    dv_roll = jnp.stack(roll_value_list, axis=2).reshape(ROLL_TOKENS, KVH, HD)
    return (dq_prompt, dk_prompt, dv_prompt, dq_roll, dk_roll, dv_roll)
```

```python
import functools
import math

import jax
import jax.numpy as jnp
from jax import lax
from jax.experimental import pallas as pl
from jax.experimental.pallas import tpu as pltpu
from jax.sharding import Mesh, PartitionSpec as P

AXES = (("zl", 8), ("x", 4), ("core", 2), ("zh", 2), ("y", 4))
CTX = ("zl", "x", "core")
GRP = ("zh", "y")
FAR = ("zl", "zh", "y")
NEAR = ("x", "core")
X, CORES, ZL = 4, 2, 8
BLOCKS = X * CORES

HD = 128
TOKENS = 64
ROWS = 512
KEYS = ZL * TOKENS
MASKED = -1e30
SCALING = 1.0 / math.sqrt(HD)
LOG2E = math.log2(math.e)
SCALE2 = SCALING * LOG2E
F32 = jnp.float32
BF16 = jnp.bfloat16
NT = (((1,), (1,)), ((), ()))


def shifted(value, axis, steps):
    count = lax.axis_size(axis)
    return lax.ppermute(value, axis, [(i, (i + steps) % count) for i in range(count)])


def place(step, info):
    block, kind = step // 2, step % 2
    owner_x = (info[0] + X - block % X) % X
    owner_core = (info[1] + block // X) % CORES
    return owner_x, owner_core, kind


def stats_index(step, info):
    owner_x, owner_core, kind = place(step, info)
    return (owner_x * CORES + owner_core) * 2 + kind


def load_rows(step, rows_refs, q_s, g_s):
    block = step // 2
    for i in range(BLOCKS):

        @pl.when(block == i)
        def _():
            q_s[...] = rows_refs[2 * i][0]
            g_s[...] = rows_refs[2 * i + 1][0]


def prompt_scores(step, info, keys, queries):
    owner_x, owner_core, kind = place(step, info)
    scores = lax.dot_general(keys, queries, NT, preferred_element_type=F32) * SCALE2
    key = lax.broadcasted_iota(jnp.int32, (KEYS, 1), 0)
    key_pos = (key // TOKENS) * (BLOCKS * TOKENS) + key % TOKENS + (info[0] * CORES + info[1]) * TOKENS
    row = lax.broadcasted_iota(jnp.int32, (1, ROWS), 1)
    first = ((info[2] * X + owner_x) * CORES + owner_core) * TOKENS
    limit = jnp.where(kind == 1, info[3] - 1, first + row // 8)
    return jnp.where(key_pos <= limit, scores, MASKED)


def roll_scores(step, info, keys, queries):
    owner_x, owner_core, _ = place(step, info)
    scores = lax.dot_general(keys, queries, NT, preferred_element_type=F32) * SCALE2
    key_pos = lax.broadcasted_iota(jnp.int32, (TOKENS, 1), 0) + (info[0] * CORES + info[1]) * TOKENS
    row = lax.broadcasted_iota(jnp.int32, (1, ROWS), 1)
    limit = (owner_x * CORES + owner_core) * TOKENS + row // 8
    return jnp.where(key_pos <= limit, scores, MASKED)


def sees_roll(step, info):
    owner_x, _, kind = place(step, info)
    return (kind == 1) & (owner_x // 2 == info[0] // 2)


def partial_stats(scores, weight_grad):
    top = jnp.max(scores, axis=0, keepdims=True)
    weights = jnp.exp2(scores - top)
    total = jnp.sum(weights, axis=0, keepdims=True)
    product = jnp.sum(weights * weight_grad, axis=0, keepdims=True)
    return top + jnp.log2(total), product / total


def merged(first, second):
    (log_a, delta_a), (log_b, delta_b) = first, second
    top = jnp.maximum(log_a, log_b)
    share_a, share_b = jnp.exp2(log_a - top), jnp.exp2(log_b - top)
    total = share_a + share_b
    return top + jnp.log2(total), (delta_a * share_a + delta_b * share_b) / total


def stats_kernel(info, *refs):
    rows_refs, (kv_ref, rkv_ref, stats_ref, q_s, g_s) = refs[: 4 * BLOCKS // 2], refs[4 * BLOCKS // 2 :]
    step = pl.program_id(0)
    load_rows(step, rows_refs, q_s, g_s)
    queries, grads = q_s[...], g_s[...]
    scores = prompt_scores(step, info, kv_ref[:, :HD], queries)
    weight_grad = lax.dot_general(kv_ref[:, HD:], grads, NT, preferred_element_type=F32)
    stats = partial_stats(scores, weight_grad)
    stats_ref[0, 0:1, :] = stats[0]
    stats_ref[0, 1:2, :] = stats[1]

    @pl.when(sees_roll(step, info))
    def _():
        roll = roll_scores(step, info, rkv_ref[:, :HD], queries)
        roll_grad = lax.dot_general(rkv_ref[:, HD:], grads, NT, preferred_element_type=F32)
        both = merged(stats, partial_stats(roll, roll_grad))
        stats_ref[0, 0:1, :] = both[0]
        stats_ref[0, 1:2, :] = both[1]


def block_grads(scores, weight_grad, log_total, delta, queries, grads, keys_t):
    weights = jnp.exp2(scores - log_total)
    rounded = weights.astype(BF16)
    score_grad = (weights * (weight_grad - delta)).astype(BF16)
    key_part = jnp.dot(score_grad, queries, preferred_element_type=F32) * SCALING
    value_part = jnp.dot(rounded, grads, preferred_element_type=F32)
    query_t = jnp.dot(keys_t, score_grad, preferred_element_type=F32)
    return query_t, key_part, value_part


def grads_kernel(info, *refs):
    rows_refs = refs[: 2 * BLOCKS]
    (stats_ref, kv_ref, kt_ref, rkv_ref, rkt_ref, dq0_ref, dq1_ref, dkv_ref, drkv_ref, q_s, g_s, dqt_s, acc, roll_acc) = refs[
        2 * BLOCKS :
    ]
    step = pl.program_id(0)

    @pl.when(step == 0)
    def _():
        acc[...] = jnp.zeros_like(acc)
        roll_acc[...] = jnp.zeros_like(roll_acc)

    load_rows(step, rows_refs, q_s, g_s)
    queries, grads = q_s[...], g_s[...]
    logs, deltas = stats_ref[:, 0, 0, :], stats_ref[:, 0, 1, :]
    top = jnp.max(logs, axis=0, keepdims=True)
    shares = jnp.exp2(logs - top)
    total = jnp.sum(shares, axis=0, keepdims=True)
    log_total = top + jnp.log2(total)
    delta = jnp.sum(shares * deltas, axis=0, keepdims=True) / total
    scores = prompt_scores(step, info, kv_ref[:, :HD], queries)
    weight_grad = lax.dot_general(kv_ref[:, HD:], grads, NT, preferred_element_type=F32)
    query_t, key_part, value_part = block_grads(scores, weight_grad, log_total, delta, queries, grads, kt_ref[...])
    dqt_s[...] = query_t
    acc[:, :HD] += key_part
    acc[:, HD:] += value_part

    @pl.when(sees_roll(step, info))
    def _():
        roll = roll_scores(step, info, rkv_ref[:, :HD], queries)
        roll_grad = lax.dot_general(rkv_ref[:, HD:], grads, NT, preferred_element_type=F32)
        query_r, key_r, value_r = block_grads(roll, roll_grad, log_total, delta, queries, grads, rkt_ref[...])
        dqt_s[...] += query_r
        roll_acc[:, :HD] += key_r
        roll_acc[:, HD:] += value_r

    out = (dqt_s[...] * SCALING).T.astype(BF16)

    @pl.when(step < BLOCKS)
    def _():
        dq0_ref[0] = out

    @pl.when(step >= BLOCKS)
    def _():
        dq1_ref[0] = out

    @pl.when(step == 2 * BLOCKS - 1)
    def _():
        dkv_ref[...] = acc[...].astype(BF16)
        drkv_ref[...] = roll_acc[...].astype(BF16)


def row_specs():
    def spec(block, part):
        return pl.BlockSpec((1, ROWS, HD), lambda i, info: (part + jnp.clip(i - 2 * block, 0, 1), 0, 0))

    return [spec(block, part) for block in range(BLOCKS) for part in (0, 2)]


def whole(*shape):
    return pl.BlockSpec(shape, lambda i, info: (0,) * len(shape))


COST = 2 * 8192 * 576 * HD


def call_stats(info, rows, kv, rkv):
    return pl.pallas_call(
        stats_kernel,
        out_shape=jax.ShapeDtypeStruct((2 * BLOCKS, 2, ROWS), F32),
        grid_spec=pltpu.PrefetchScalarGridSpec(
            num_scalar_prefetch=1,
            grid=(2 * BLOCKS,),
            in_specs=row_specs() + [whole(KEYS, 2 * HD), whole(TOKENS, 2 * HD)],
            out_specs=pl.BlockSpec((1, 2, ROWS), lambda i, info: (stats_index(i, info), 0, 0)),
            scratch_shapes=[pltpu.VMEM((ROWS, HD), BF16), pltpu.VMEM((ROWS, HD), BF16)],
        ),
        compiler_params=pltpu.CompilerParams(vmem_limit_bytes=40 * 2**20),
        cost_estimate=pl.CostEstimate(flops=2 * COST, bytes_accessed=5 * 2**20, transcendentals=8192 * 576),
        name="row_stats",
    )(info, *[r for r in rows for _ in (0, 1)], kv, rkv)


def call_grads(info, rows, stats, kv, kt, rkv, rkt):
    half = (BLOCKS, ROWS, HD)
    return pl.pallas_call(
        grads_kernel,
        out_shape=(
            jax.ShapeDtypeStruct(half, BF16),
            jax.ShapeDtypeStruct(half, BF16),
            jax.ShapeDtypeStruct((KEYS, 2 * HD), BF16),
            jax.ShapeDtypeStruct((TOKENS, 2 * HD), BF16),
        ),
        grid_spec=pltpu.PrefetchScalarGridSpec(
            num_scalar_prefetch=1,
            grid=(2 * BLOCKS,),
            in_specs=row_specs()
            + [
                pl.BlockSpec((BLOCKS, 1, 2, ROWS), lambda i, info: (0, stats_index(i, info), 0, 0)),
                whole(KEYS, 2 * HD),
                whole(HD, KEYS),
                whole(TOKENS, 2 * HD),
                whole(HD, TOKENS),
            ],
            out_specs=(
                pl.BlockSpec((1, ROWS, HD), lambda i, info: (jnp.minimum(i, BLOCKS - 1), 0, 0)),
                pl.BlockSpec((1, ROWS, HD), lambda i, info: (jnp.maximum(i - BLOCKS, 0), 0, 0)),
                whole(KEYS, 2 * HD),
                whole(TOKENS, 2 * HD),
            ),
            scratch_shapes=[
                pltpu.VMEM((ROWS, HD), BF16),
                pltpu.VMEM((ROWS, HD), BF16),
                pltpu.VMEM((HD, ROWS), F32),
                pltpu.VMEM((KEYS, 2 * HD), F32),
                pltpu.VMEM((TOKENS, 2 * HD), F32),
            ],
        ),
        compiler_params=pltpu.CompilerParams(vmem_limit_bytes=40 * 2**20),
        cost_estimate=pl.CostEstimate(flops=5 * COST, bytes_accessed=8 * 2**20, transcendentals=8192 * 576),
        name="row_grads",
    )(info, *[r for r in rows for _ in (0, 1)], stats, kv, kt, rkv, rkt)


def per_device(q_prompt, k_prompt, v_prompt, grad_prompt, q_roll, k_roll, v_roll, grad_roll, prompt_len, roll_len):
    zl, x, core = (lax.axis_index(name) for name in CTX)
    ctx = (zl * X + x) * CORES + core
    pair = jnp.transpose(jnp.concatenate([k_prompt, v_prompt], axis=-1), (1, 0, 2))
    sent = jnp.broadcast_to(pair[None], (ZL,) + pair.shape).reshape(ZL * pair.shape[0], *pair.shape[1:])
    kv = lax.all_to_all(sent, FAR, split_axis=0, concat_axis=0, tiled=True).reshape(KEYS, 2 * HD)
    token = jnp.arange(TOKENS, dtype=jnp.int32)
    roll_limit = lax.dynamic_index_in_dim(roll_len, ctx // 4, 0, keepdims=False)
    prompt_keep = (ctx * TOKENS + token < prompt_len[0]).astype(BF16)[:, None, None]
    roll_keep = ((ctx % 4) * TOKENS + token < roll_limit).astype(BF16)[:, None, None]
    own = jnp.stack([q_prompt, q_roll, grad_prompt * prompt_keep, grad_roll * roll_keep]).reshape(4, ROWS, HD)
    rows = [own] + [shifted(own, "x", steps) for steps in range(1, X)]
    rows = rows + [shifted(r, "core", 1) for r in rows]
    rkv = jnp.concatenate([k_roll, v_roll], axis=-1).reshape(TOKENS, 2 * HD)
    info = jnp.stack([x, core, zl, prompt_len[0]]).astype(jnp.int32)
    stats = call_stats(info, rows, kv, rkv)
    stats = lax.all_to_all(
        jnp.broadcast_to(stats[None], (BLOCKS,) + stats.shape), NEAR, split_axis=0, concat_axis=0, tiled=True
    )
    dq_same, dq_other, dkv, drkv = call_grads(info, rows, stats, kv, kv[:, :HD].T, rkv, rkv[:, :HD].T)
    groups = k_prompt.shape[1]
    back = lax.all_to_all(
        dkv.reshape(ZL * groups, TOKENS // groups, 2 * HD), FAR, split_axis=0, concat_axis=0, tiled=True
    )
    summed = jnp.sum(back.reshape(ZL, groups, TOKENS // groups, 2 * HD).astype(F32), axis=0)
    returned = jnp.transpose(summed.astype(BF16), (1, 0, 2))
    arrived = shifted(dq_other, "core", 1)
    halves = (dq_same.astype(F32) + arrived.astype(F32)).astype(BF16).reshape(X, 2 * ROWS, HD)
    total = halves[0].astype(F32)
    for steps in range(1, X):
        total = total + shifted(halves[steps], "x", -steps).astype(F32)
    dq = total.astype(BF16).reshape(2, TOKENS, ROWS // TOKENS, HD)
    drkv = drkv.reshape(TOKENS, 1, 2 * HD)
    return (dq[0], returned[..., :HD], returned[..., HD:], dq[1], drkv[..., :HD], drkv[..., HD:])


def solution(mesh):
    names = tuple(name for name, _ in AXES)
    fine = Mesh(mesh.devices.reshape([size for _, size in AXES]), names)
    by_head, by_token = P(CTX, GRP, None), P(CTX + GRP, None, None)
    return jax.shard_map(
        per_device,
        mesh=fine,
        in_specs=(by_head, by_token, by_token, by_head, by_head, by_head, by_head, by_head, P(), P()),
        out_specs=(by_head, by_token, by_token, by_head, by_head, by_head),
        check_vma=False,
    )
```

```python
import math

import jax
import jax.numpy as jnp
from jax import lax
from jax.experimental import pallas as pl
from jax.experimental.pallas import tpu as pltpu
from jax.sharding import Mesh, PartitionSpec as P

AXES = (("zl", 8), ("x", 4), ("core", 2), ("zh", 2), ("y", 4))
CTX = ("zl", "x", "core")
GRP = ("zh", "y")
FAR = ("zl", "zh", "y")
NEAR = ("x", "core")
X, CORES, ZL = 4, 2, 8
BLOCKS = X * CORES

HD = 128
TOKENS = 64
ROWS = 512
KEYS = ZL * TOKENS
MASKED = -1e30
SCALING = 1.0 / math.sqrt(HD)
LOG2E = math.log2(math.e)
SCALE2 = SCALING * LOG2E
F32 = jnp.float32
BF16 = jnp.bfloat16
NT = (((1,), (1,)), ((), ()))


def shifted(value, axis, steps):
    count = lax.axis_size(axis)
    return lax.ppermute(value, axis, [(i, (i + steps) % count) for i in range(count)])


def owner(block, info):
    return (info[0] + X - block % X) % X, (info[1] + block // X) % CORES


def first_tokens(block, kind, info):
    owner_x, owner_core = owner(block, info)
    in_prompt = ((info[2] * X + owner_x) * CORES + owner_core) * TOKENS
    in_roll = ((owner_x % 2) * CORES + owner_core) * TOKENS
    roll = kind == 1
    return jnp.where(roll, in_roll, in_prompt), jnp.where(roll, info[4 + info[2] * 2 + owner_x // 2], info[3])


def row_tokens():
    return lax.broadcasted_iota(jnp.int32, (1, ROWS), 1) // 8


def prompt_scores(block, kind, info, keys, queries):
    scores = lax.dot_general(keys, queries, NT, preferred_element_type=F32) * SCALE2
    key = lax.broadcasted_iota(jnp.int32, (KEYS, 1), 0)
    key_pos = (key // TOKENS) * (BLOCKS * TOKENS) + key % TOKENS + (info[0] * CORES + info[1]) * TOKENS
    limit = jnp.where(kind == 1, info[3] - 1, first_tokens(block, 0, info)[0] + row_tokens())
    return jnp.where(key_pos <= limit, scores, MASKED)


def roll_scores(block, info, keys, queries):
    scores = lax.dot_general(keys, queries, NT, preferred_element_type=F32) * SCALE2
    key_pos = lax.broadcasted_iota(jnp.int32, (TOKENS, 1), 0) + ((info[0] % 2) * CORES + info[1]) * TOKENS
    return jnp.where(key_pos <= first_tokens(block, 1, info)[0] + row_tokens(), scores, MASKED)


def partial_stats(scores, weight_grad):
    top = jnp.max(scores, axis=0, keepdims=True)
    weights = jnp.exp2(scores - top)
    total = jnp.sum(weights, axis=0, keepdims=True)
    product = jnp.sum(weights * weight_grad, axis=0, keepdims=True)
    return top + jnp.log2(total), product / total


def merged(first, second):
    (log_a, delta_a), (log_b, delta_b) = first, second
    top = jnp.maximum(log_a, log_b)
    share_a, share_b = jnp.exp2(log_a - top), jnp.exp2(log_b - top)
    total = share_a + share_b
    return top + jnp.log2(total), (delta_a * share_a + delta_b * share_b) / total


def fetch(refs, rows_s, sems):
    for i, ref in enumerate(refs):
        pltpu.make_async_copy(ref, rows_s.at[i], sems.at[i]).start()


def arrive(i, refs, rows_s, sems):
    pltpu.make_async_copy(refs[0], rows_s.at[i], sems.at[i]).wait()


def sees_roll(block, kind, info):
    return (kind == 1) & (owner(block, info)[0] // 2 == info[0] // 2)


def block_stats(block, kind, info, queries, grads, kv_ref, rk_ref, rv_ref, out_ref):
    def put(stats):
        out_ref[pl.ds(2 * kind, 1), :] = stats[0]
        out_ref[pl.ds(2 * kind + 1, 1), :] = stats[1]

    scores = prompt_scores(block, kind, info, kv_ref[:, :HD], queries)
    weight_grad = lax.dot_general(kv_ref[:, HD:], grads, NT, preferred_element_type=F32)
    stats = partial_stats(scores, weight_grad)
    put(stats)

    @pl.when(sees_roll(block, kind, info))
    def _():
        roll = roll_scores(block, info, rk_ref[...], queries)
        roll_grad = lax.dot_general(rv_ref[...], grads, NT, preferred_element_type=F32)
        put(merged(stats, partial_stats(roll, roll_grad)))


def own_stats_kernel(info, rows_ref, kv_ref, rk_ref, rv_ref, stats_ref):
    @pl.loop(0, 2)
    def _(kind):
        block_stats(0, kind, info, rows_ref[kind], rows_ref[2 + kind], kv_ref, rk_ref, rv_ref, stats_ref)


def stats_kernel(info, *refs):
    others, (own_ref, kv_ref, rk_ref, rv_ref, out_ref, rows_s, stats_s, sems) = refs[: BLOCKS - 1], refs[BLOCKS - 1 :]
    fetch(others, rows_s, sems)
    stats_s[info[0] * CORES + info[1]] = own_ref[...]

    @pl.loop(2, 2 * BLOCKS)
    def _(step):
        block, kind = step // 2, step % 2

        @pl.when(kind == 0)
        def _():
            arrive(block - 1, others, rows_s, sems)

        owner_x, owner_core = owner(block, info)
        rows = rows_s.at[block - 1]
        out = stats_s.at[owner_x * CORES + owner_core]
        block_stats(block, kind, info, rows[kind], rows[2 + kind], kv_ref, rk_ref, rv_ref, out)

    for peer in range(BLOCKS):
        out_ref[peer] = stats_s[...]


def combined(stats_ref, block, kind, info):
    owner_x, owner_core = owner(block, info)
    at = owner_x * CORES + owner_core
    logs = jnp.concatenate([stats_ref[i, at, pl.ds(2 * kind, 1), :] for i in range(BLOCKS)], axis=0)
    deltas = jnp.concatenate([stats_ref[i, at, pl.ds(2 * kind + 1, 1), :] for i in range(BLOCKS)], axis=0)
    top = jnp.max(logs, axis=0, keepdims=True)
    shares = jnp.exp2(logs - top)
    total = jnp.sum(shares, axis=0, keepdims=True)
    start, length = first_tokens(block, kind, info)
    log_total = jnp.where(start + row_tokens() < length, top + jnp.log2(total), -MASKED)
    return log_total, jnp.sum(shares * deltas, axis=0, keepdims=True) / total


def block_grads(scores, weight_grad, log_total, delta, queries, grads, keys_t):
    weights = jnp.exp2(scores - log_total)
    score_grad = (weights * (weight_grad - delta)).astype(BF16)
    key_part = jnp.dot(score_grad, queries, preferred_element_type=F32)
    value_part = jnp.dot(weights.astype(BF16), grads, preferred_element_type=F32)
    query_t = jnp.dot(keys_t, score_grad, preferred_element_type=F32)
    return query_t, key_part, value_part


def grads_kernel(info, *refs):
    rows = refs[:BLOCKS]
    (stats_ref, kv_ref, kt_ref, rk_ref, rkt_ref, rv_ref) = refs[BLOCKS : BLOCKS + 6]
    (dq0_ref, dq1_ref, dkv_ref, drk_ref, drv_ref, rows_s, dqt_s, acc, roll_acc, sems) = refs[BLOCKS + 6 :]
    fetch(rows, rows_s, sems)
    acc[...] = jnp.zeros_like(acc)
    roll_acc[...] = jnp.zeros_like(roll_acc)

    @pl.loop(0, 2 * BLOCKS)
    def _(step):
        block, kind = step // 2, step % 2

        @pl.when(kind == 0)
        def _():
            arrive(block, rows, rows_s, sems)

        log_total, delta = combined(stats_ref, block, kind, info)
        queries, grads = rows_s[block, kind], rows_s[block, 2 + kind]
        scores = prompt_scores(block, kind, info, kv_ref[:, :HD], queries)
        weight_grad = lax.dot_general(kv_ref[:, HD:], grads, NT, preferred_element_type=F32)
        query_t, key_part, value_part = block_grads(
            scores, weight_grad, log_total, delta, queries, grads, kt_ref[...]
        )
        dqt_s[...] = query_t
        acc[:, :HD] += key_part
        acc[:, HD:] += value_part

        @pl.when(sees_roll(block, kind, info))
        def _():
            roll = roll_scores(block, info, rk_ref[...], queries)
            roll_grad = lax.dot_general(rv_ref[...], grads, NT, preferred_element_type=F32)
            query_r, key_r, value_r = block_grads(roll, roll_grad, log_total, delta, queries, grads, rkt_ref[...])
            dqt_s[...] += query_r
            roll_acc[:, :HD] += key_r
            roll_acc[:, HD:] += value_r

        out = (dqt_s[...] * SCALING).T.astype(BF16)
        at = pl.ds(pl.multiple_of(kind * ROWS, ROWS), ROWS)

        @pl.when(block < X)
        def _():
            dq0_ref[block, at, :] = out

        @pl.when(block >= X)
        def _():
            dq1_ref[block - X, at, :] = out

    dkv_ref[:, :HD] = (acc[:, :HD] * SCALING).astype(BF16)
    dkv_ref[:, HD:] = acc[:, HD:].astype(BF16)
    drk_ref[...] = (roll_acc[:, :HD] * SCALING).astype(BF16)
    drv_ref[...] = roll_acc[:, HD:].astype(BF16)


def finish_kernel(back_ref, dk_ref, dv_ref):
    total = jnp.sum(back_ref[...].astype(F32), axis=0)
    for head in range(total.shape[0]):
        dk_ref[:, head, :] = total[head, :, :HD].astype(BF16)
        dv_ref[:, head, :] = total[head, :, HD:].astype(BF16)


VMEM = pl.BlockSpec(memory_space=pltpu.VMEM)
SMEM = pl.BlockSpec(memory_space=pltpu.SMEM)
ANY = pl.BlockSpec(memory_space=pl.ANY)
PARAMS = pltpu.CompilerParams(vmem_limit_bytes=28 * 2**20)
COST = 2 * 1024 * 576 * HD


def cost(flops, byte_count):
    return pl.CostEstimate(flops=flops, bytes_accessed=byte_count, transcendentals=0)


def call_own_stats(info, own, kv, rk, rv):
    return pl.pallas_call(
        own_stats_kernel,
        out_shape=jax.ShapeDtypeStruct((4, ROWS), F32),
        in_specs=[SMEM] + [VMEM] * 4,
        out_specs=VMEM,
        compiler_params=PARAMS,
        cost_estimate=cost(OWN_FLOPS, 2**20),
        name="row_own_stats",
    )(info, own, kv, rk, rv)


OWN_FLOPS = 100 * 10**9


def call_stats(info, others, own_stats, kv, rk, rv):
    return pl.pallas_call(
        stats_kernel,
        out_shape=jax.ShapeDtypeStruct((BLOCKS, BLOCKS, 4, ROWS), F32),
        in_specs=[SMEM] + [ANY] * (BLOCKS - 1) + [VMEM] * 4,
        out_specs=VMEM,
        scratch_shapes=[
            pltpu.VMEM((BLOCKS - 1, 4, ROWS, HD), BF16),
            pltpu.VMEM((BLOCKS, 4, ROWS), F32),
            pltpu.SemaphoreType.DMA((BLOCKS - 1,)),
        ],
        compiler_params=PARAMS,
        cost_estimate=cost(2 * 7 * COST, 4 * 2**20),
        name="row_stats",
    )(info, *others, own_stats, kv, rk, rv)


def call_grads(info, rows, stats, kv, kt, rk, rkt, rv):
    half = jax.ShapeDtypeStruct((X, 2 * ROWS, HD), BF16)
    roll = jax.ShapeDtypeStruct((TOKENS, HD), BF16)
    return pl.pallas_call(
        grads_kernel,
        out_shape=(half, half, jax.ShapeDtypeStruct((KEYS, 2 * HD), BF16), roll, roll),
        in_specs=[SMEM] + [ANY] * BLOCKS + [VMEM] * 6,
        out_specs=(VMEM,) * 5,
        scratch_shapes=[
            pltpu.VMEM((BLOCKS, 4, ROWS, HD), BF16),
            pltpu.VMEM((HD, ROWS), F32),
            pltpu.VMEM((KEYS, 2 * HD), F32),
            pltpu.VMEM((TOKENS, 2 * HD), F32),
            pltpu.SemaphoreType.DMA((BLOCKS,)),
        ],
        compiler_params=PARAMS,
        cost_estimate=cost(5 * 8 * COST, 7 * 2**20),
        name="row_grads",
    )(info, *rows, stats, kv, kt, rk, rkt, rv)


def call_finish(back):
    tokens, heads = back.shape[2], back.shape[1]
    out = jax.ShapeDtypeStruct((tokens, heads, HD), BF16)
    return pl.pallas_call(
        finish_kernel, out_shape=(out, out), in_specs=[VMEM], out_specs=(VMEM, VMEM), name="sum_planes"
    )(back)


def per_device(q_prompt, k_prompt, v_prompt, grad_prompt, q_roll, k_roll, v_roll, grad_roll, prompt_len, roll_len):
    zl, x, core = (lax.axis_index(name) for name in CTX)
    pair = jnp.transpose(jnp.concatenate([k_prompt, v_prompt], axis=-1), (1, 0, 2))
    sent = jnp.broadcast_to(pair[None], (ZL,) + pair.shape).reshape(ZL * pair.shape[0], *pair.shape[1:])
    kv = lax.all_to_all(sent, FAR, split_axis=0, concat_axis=0, tiled=True).reshape(KEYS, 2 * HD)
    own = jnp.stack([q_prompt, q_roll, grad_prompt, grad_roll]).reshape(4, ROWS, HD)
    rows = [own] + [shifted(own, "x", steps) for steps in range(1, X)]
    rows = rows + [shifted(r, "core", 1) for r in rows]
    rk, rv = k_roll.reshape(TOKENS, HD), v_roll.reshape(TOKENS, HD)
    info = jnp.concatenate([jnp.stack([x, core, zl]).astype(jnp.int32), prompt_len, roll_len])
    own_stats = call_own_stats(info, own, kv, rk, rv)
    stats = call_stats(info, rows[1:], own_stats, kv, rk, rv)
    stats = lax.all_to_all(stats, NEAR, split_axis=0, concat_axis=0, tiled=True)
    dq_same, dq_other, dkv, drk, drv = call_grads(info, rows, stats, kv, kv[:, :HD].T, rk, rk.T, rv)
    groups = k_prompt.shape[1]
    back = lax.all_to_all(
        dkv.reshape(ZL * groups, TOKENS // groups, 2 * HD), FAR, split_axis=0, concat_axis=0, tiled=True
    )
    dk_prompt, dv_prompt = call_finish(back.reshape(ZL, groups, TOKENS // groups, 2 * HD))
    arrived = shifted(dq_other, "core", 1)
    halves = (dq_same.astype(F32) + arrived.astype(F32)).astype(BF16)
    parts = [halves[0]] + [shifted(halves[steps], "x", -steps) for steps in range(1, X)]
    dq = [
        sum(part[first : first + ROWS].astype(F32) for part in parts).astype(BF16).reshape(q_prompt.shape)
        for first in (0, ROWS)
    ]
    return (dq[0], dk_prompt, dv_prompt, dq[1], drk.reshape(k_roll.shape), drv.reshape(v_roll.shape))


def solution(mesh):
    names = tuple(name for name, _ in AXES)
    fine = Mesh(mesh.devices.reshape([size for _, size in AXES]), names)
    by_head, by_token = P(CTX, GRP, None), P(CTX + GRP, None, None)
    return jax.shard_map(
        per_device,
        mesh=fine,
        in_specs=(by_head, by_token, by_token, by_head, by_head, by_head, by_head, by_head, P(), P()),
        out_specs=(by_head, by_token, by_token, by_head, by_head, by_head),
        check_vma=False,
    )
```

```python
import math

import jax
import jax.numpy as jnp
from jax import lax
from jax.experimental import pallas as pl
from jax.experimental.pallas import tpu as pltpu
from jax.sharding import Mesh, PartitionSpec as P

AXES = (("zl", 8), ("x", 4), ("core", 2), ("zh", 2), ("y", 4))
CTX = ("zl", "x", "core")
GRP = ("zh", "y")
FAR = ("zl", "zh", "y")
NEAR = ("x", "core")
X, CORES, ZL = 4, 2, 8
BLOCKS = X * CORES

HD = 128
TOKENS = 64
ROWS = 512
KEYS = ZL * TOKENS
MASKED = -1e30
SCALING = 1.0 / math.sqrt(HD)
LOG2E = math.log2(math.e)
SCALE2 = SCALING * LOG2E
F32 = jnp.float32
BF16 = jnp.bfloat16
NT = (((1,), (1,)), ((), ()))


def shifted(value, axis, steps):
    count = lax.axis_size(axis)
    return lax.ppermute(value, axis, [(i, (i + steps) % count) for i in range(count)])


def owner(block, info):
    return (info[0] + X - block % X) % X, (info[1] + block // X) % CORES


def first_tokens(block, kind, info):
    owner_x, owner_core = owner(block, info)
    if kind == 0:
        return ((info[2] * X + owner_x) * CORES + owner_core) * TOKENS, info[3]
    return ((owner_x % 2) * CORES + owner_core) * TOKENS, info[4 + info[2] * 2 + owner_x // 2]


def row_tokens():
    return lax.broadcasted_iota(jnp.int32, (1, ROWS), 1) // 8


def prompt_scores(block, kind, info, keys, queries):
    scores = lax.dot_general(keys, queries, NT, preferred_element_type=F32) * SCALE2
    key = lax.broadcasted_iota(jnp.int32, (KEYS, 1), 0)
    key_pos = (key // TOKENS) * (BLOCKS * TOKENS) + key % TOKENS + (info[0] * CORES + info[1]) * TOKENS
    if kind == 1:
        limit = jnp.zeros((1, ROWS), jnp.int32) + (info[3] - 1)
    else:
        limit = first_tokens(block, 0, info)[0] + row_tokens()
    return jnp.where(key_pos <= limit, scores, MASKED)


def roll_scores(block, info, keys, queries):
    scores = lax.dot_general(keys, queries, NT, preferred_element_type=F32) * SCALE2
    key_pos = lax.broadcasted_iota(jnp.int32, (TOKENS, 1), 0) + ((info[0] % 2) * CORES + info[1]) * TOKENS
    return jnp.where(key_pos <= first_tokens(block, 1, info)[0] + row_tokens(), scores, MASKED)


def partial_stats(scores, weight_grad):
    top = jnp.max(scores, axis=0, keepdims=True)
    weights = jnp.exp2(scores - top)
    total = jnp.sum(weights, axis=0, keepdims=True)
    product = jnp.sum(weights * weight_grad, axis=0, keepdims=True)
    return top + jnp.log2(total), product / total


def merged(first, second):
    (log_a, delta_a), (log_b, delta_b) = first, second
    top = jnp.maximum(log_a, log_b)
    share_a, share_b = jnp.exp2(log_a - top), jnp.exp2(log_b - top)
    total = share_a + share_b
    return top + jnp.log2(total), (delta_a * share_a + delta_b * share_b) / total


def fetch(refs, rows_s, sems):
    for i, ref in enumerate(refs):
        pltpu.make_async_copy(ref, rows_s.at[i], sems.at[i]).start()


def arrive(i, refs, rows_s, sems):
    pltpu.make_async_copy(refs[0], rows_s.at[i], sems.at[i]).wait()


def sees_roll(block, info):
    return owner(block, info)[0] // 2 == info[0] // 2


def stats_kernel(info, *refs):
    rows, (kv_ref, rkv_ref, out_ref, all_ref, rows_s, stats_s, sems, out_sems) = refs[:BLOCKS], refs[BLOCKS:]
    fetch(rows, rows_s, sems)

    def keep(block):
        return pltpu.make_async_copy(rows_s.at[block], all_ref.at[block], out_sems.at[block])

    @pl.loop(0, BLOCKS)
    def _(block):
        arrive(block, rows, rows_s, sems)
        keep(block).start()
        owner_x, owner_core = owner(block, info)
        at = owner_x * CORES + owner_core

        def put(kind, stats):
            stats_s[at, 2 * kind : 2 * kind + 1, :] = stats[0]
            stats_s[at, 2 * kind + 1 : 2 * kind + 2, :] = stats[1]

        for kind in (0, 1):
            queries, grads = rows_s[block, kind], rows_s[block, 2 + kind]
            scores = prompt_scores(block, kind, info, kv_ref[:, :HD], queries)
            weight_grad = lax.dot_general(kv_ref[:, HD:], grads, NT, preferred_element_type=F32)
            put(kind, partial_stats(scores, weight_grad))

        @pl.when(sees_roll(block, info))
        def _():
            roll = roll_scores(block, info, rkv_ref[:, :HD], rows_s[block, 1])
            roll_grad = lax.dot_general(rkv_ref[:, HD:], rows_s[block, 3], NT, preferred_element_type=F32)
            put(1, merged((stats_s[at, 2:3, :], stats_s[at, 3:4, :]), partial_stats(roll, roll_grad)))

    for peer in range(BLOCKS):
        out_ref[peer] = stats_s[...]
    for block in range(BLOCKS):
        keep(block).wait()


def combined(stats_ref, block, kind, info):
    owner_x, owner_core = owner(block, info)
    at = owner_x * CORES + owner_core
    logs, deltas = stats_ref[:, at, 2 * kind, :], stats_ref[:, at, 2 * kind + 1, :]
    top = jnp.max(logs, axis=0, keepdims=True)
    shares = jnp.exp2(logs - top)
    total = jnp.sum(shares, axis=0, keepdims=True)
    start, length = first_tokens(block, kind, info)
    log_total = jnp.where(start + row_tokens() < length, top + jnp.log2(total), -MASKED)
    return log_total, jnp.sum(shares * deltas, axis=0, keepdims=True) / total


def block_grads(scores, weight_grad, log_total, delta, queries, grads, keys_t):
    weights = jnp.exp2(scores - log_total)
    score_grad = (weights * (weight_grad - delta)).astype(BF16)
    key_part = jnp.dot(score_grad, queries, preferred_element_type=F32)
    value_part = jnp.dot(weights.astype(BF16), grads, preferred_element_type=F32)
    query_t = jnp.dot(keys_t, score_grad, preferred_element_type=F32)
    return query_t, key_part, value_part


def grads_kernel(info, rows_ref, stats_ref, kv_ref, kt_ref, rkv_ref, rkt_ref, *refs):
    (dq0_ref, dq1_ref, dkv_ref, drk_ref, drv_ref, rows_s, dqt_s, acc, roll_acc, sems) = refs
    rows = [rows_ref.at[block] for block in range(BLOCKS)]
    fetch(rows, rows_s, sems)
    acc[...] = jnp.zeros_like(acc)
    roll_acc[...] = jnp.zeros_like(roll_acc)

    @pl.loop(0, BLOCKS)
    def _(block):
        arrive(block, rows, rows_s, sems)
        for kind in (0, 1):
            log_total, delta = combined(stats_ref, block, kind, info)
            queries, grads = rows_s[block, kind], rows_s[block, 2 + kind]
            scores = prompt_scores(block, kind, info, kv_ref[:, :HD], queries)
            weight_grad = lax.dot_general(kv_ref[:, HD:], grads, NT, preferred_element_type=F32)
            query_t, key_part, value_part = block_grads(
                scores, weight_grad, log_total, delta, queries, grads, kt_ref[...]
            )
            dqt_s[kind] = query_t
            acc[:, :HD] += key_part
            acc[:, HD:] += value_part

        @pl.when(sees_roll(block, info))
        def _():
            log_total, delta = combined(stats_ref, block, 1, info)
            queries, grads = rows_s[block, 1], rows_s[block, 3]
            roll = roll_scores(block, info, rkv_ref[:, :HD], queries)
            roll_grad = lax.dot_general(rkv_ref[:, HD:], grads, NT, preferred_element_type=F32)
            query_r, key_r, value_r = block_grads(roll, roll_grad, log_total, delta, queries, grads, rkt_ref[...])
            dqt_s[1] += query_r
            roll_acc[:, :HD] += key_r
            roll_acc[:, HD:] += value_r

        for kind in (0, 1):
            out = (dqt_s[kind] * SCALING).T.astype(BF16)
            at = slice(kind * ROWS, kind * ROWS + ROWS)

            @pl.when(block < X)
            def _():
                dq0_ref[block, at, :] = out

            @pl.when(block >= X)
            def _():
                dq1_ref[block - X, at, :] = out

    dkv_ref[:, :HD] = (acc[:, :HD] * SCALING).astype(BF16)
    dkv_ref[:, HD:] = acc[:, HD:].astype(BF16)
    drk_ref[...] = (roll_acc[:, :HD] * SCALING).astype(BF16)
    drv_ref[...] = roll_acc[:, HD:].astype(BF16)


def finish_kernel(back_ref, dk_ref, dv_ref):
    total = jnp.sum(back_ref[...].astype(F32), axis=0)
    for head in range(total.shape[0]):
        dk_ref[:, head, :] = total[head, :, :HD].astype(BF16)
        dv_ref[:, head, :] = total[head, :, HD:].astype(BF16)


VMEM = pl.BlockSpec(memory_space=pltpu.VMEM)
SMEM = pl.BlockSpec(memory_space=pltpu.SMEM)
HBM = pl.BlockSpec(memory_space=pltpu.HBM)
PARAMS = pltpu.CompilerParams(vmem_limit_bytes=52 * 2**20)
COST = 2 * 1024 * 576 * HD


WAIT_FLOPS = 100 * 10**9


def cost(flops, byte_count):
    return pl.CostEstimate(flops=flops, bytes_accessed=byte_count, transcendentals=0)


def call_stats(info, rows, kv, rkv):
    return pl.pallas_call(
        stats_kernel,
        out_shape=(
            jax.ShapeDtypeStruct((BLOCKS, BLOCKS, 4, ROWS), F32),
            jax.ShapeDtypeStruct((BLOCKS, 4, ROWS, HD), BF16),
        ),
        in_specs=[SMEM] + [HBM] * BLOCKS + [VMEM] * 2,
        out_specs=(VMEM, HBM),
        scratch_shapes=[
            pltpu.VMEM((BLOCKS, 4, ROWS, HD), BF16),
            pltpu.VMEM((BLOCKS, 4, ROWS), F32),
            pltpu.SemaphoreType.DMA((BLOCKS,)),
            pltpu.SemaphoreType.DMA((BLOCKS,)),
        ],
        compiler_params=PARAMS,
        cost_estimate=cost(2 * 8 * COST, 5 * 2**20),
        name="row_stats",
    )(info, *rows, kv, rkv)


def call_grads(info, rows, stats, kv, kt, rkv, rkt):
    half = jax.ShapeDtypeStruct((X, 2 * ROWS, HD), BF16)
    roll = jax.ShapeDtypeStruct((TOKENS, HD), BF16)
    return pl.pallas_call(
        grads_kernel,
        out_shape=(half, half, jax.ShapeDtypeStruct((KEYS, 2 * HD), BF16), roll, roll),
        in_specs=[SMEM, HBM] + [VMEM] * 5,
        out_specs=(VMEM,) * 5,
        scratch_shapes=[
            pltpu.VMEM((BLOCKS, 4, ROWS, HD), BF16),
            pltpu.VMEM((2, HD, ROWS), F32),
            pltpu.VMEM((KEYS, 2 * HD), F32),
            pltpu.VMEM((TOKENS, 2 * HD), F32),
            pltpu.SemaphoreType.DMA((BLOCKS,)),
        ],
        compiler_params=PARAMS,
        cost_estimate=cost(5 * 8 * COST, 7 * 2**20),
        name="row_grads",
    )(info, rows, stats, kv, kt, rkv, rkt)


def call_finish(back):
    tokens, heads = back.shape[2], back.shape[1]
    out = jax.ShapeDtypeStruct((tokens, heads, HD), BF16)
    return pl.pallas_call(
        finish_kernel,
        out_shape=(out, out),
        in_specs=[VMEM],
        out_specs=(VMEM, VMEM),
        compiler_params=pltpu.CompilerParams(vmem_limit_bytes=4 * 2**20),
        cost_estimate=cost(WAIT_FLOPS, 2**18),
        name="sum_planes",
    )(back)


def per_device(q_prompt, k_prompt, v_prompt, grad_prompt, q_roll, k_roll, v_roll, grad_roll, prompt_len, roll_len):
    zl, x, core = (lax.axis_index(name) for name in CTX)
    pair = jnp.transpose(jnp.concatenate([k_prompt, v_prompt], axis=-1), (1, 0, 2))
    sent = jnp.broadcast_to(pair[None], (ZL,) + pair.shape).reshape(ZL * pair.shape[0], *pair.shape[1:])
    kv = lax.all_to_all(sent, FAR, split_axis=0, concat_axis=0, tiled=True).reshape(KEYS, 2 * HD)
    own = jnp.stack([q_prompt, q_roll, grad_prompt, grad_roll]).reshape(4, ROWS, HD)
    rows = [own] + [shifted(own, "x", steps) for steps in range(1, X)]
    rows = rows + [shifted(r, "core", 1) for r in rows]
    rkv = jnp.concatenate([k_roll, v_roll], axis=-1).reshape(TOKENS, 2 * HD)
    info = jnp.concatenate([jnp.stack([x, core, zl]).astype(jnp.int32), prompt_len, roll_len])
    stats, rows = call_stats(info, rows, kv, rkv)
    stats = lax.all_to_all(stats, NEAR, split_axis=0, concat_axis=0, tiled=True)
    dq_same, dq_other, dkv, drk, drv = call_grads(info, rows, stats, kv, kv[:, :HD].T, rkv, rkv[:, :HD].T)
    groups = k_prompt.shape[1]
    back = lax.all_to_all(
        dkv.reshape(ZL * groups, TOKENS // groups, 2 * HD), FAR, split_axis=0, concat_axis=0, tiled=True
    )
    dk_prompt, dv_prompt = call_finish(back.reshape(ZL, groups, TOKENS // groups, 2 * HD))
    arrived = shifted(dq_other, "core", 1)
    halves = (dq_same.astype(F32) + arrived.astype(F32)).astype(BF16)
    parts = [halves[0]] + [shifted(halves[steps], "x", -steps) for steps in range(1, X)]
    dq = [
        sum(part[first : first + ROWS].astype(F32) for part in parts).astype(BF16).reshape(q_prompt.shape)
        for first in (0, ROWS)
    ]
    return (dq[0], dk_prompt, dv_prompt, dq[1], drk.reshape(k_roll.shape), drv.reshape(v_roll.shape))


def solution(mesh):
    names = tuple(name for name, _ in AXES)
    fine = Mesh(mesh.devices.reshape([size for _, size in AXES]), names)
    by_head, by_token = P(CTX, GRP, None), P(CTX + GRP, None, None)
    return jax.shard_map(
        per_device,
        mesh=fine,
        in_specs=(by_head, by_token, by_token, by_head, by_head, by_head, by_head, by_head, P(), P()),
        out_specs=(by_head, by_token, by_token, by_head, by_head, by_head),
        check_vma=False,
    )
```

```python
import math

import jax
import jax.numpy as jnp
from jax import lax
from jax.experimental import pallas as pl
from jax.experimental.pallas import tpu as pltpu
from jax.sharding import Mesh, PartitionSpec as P

AXES = (("zl", 8), ("x", 4), ("core", 2), ("zh", 2), ("y", 4))
CTX = ("zl", "x", "core")
GRP = ("zh", "y")
FAR = ("zl", "zh", "y")
NEAR = ("x", "core")
X, CORES, ZL = 4, 2, 8
BLOCKS = X * CORES

HD = 128
TOKENS = 64
ROWS = 512
KEYS = ZL * TOKENS
SHORT_KEYS = 6 * TOKENS
MASKED = -1e30
SCALING = 1.0 / math.sqrt(HD)
LOG2E = math.log2(math.e)
SCALE2 = SCALING * LOG2E
F32 = jnp.float32
BF16 = jnp.bfloat16
NT = (((1,), (1,)), ((), ()))


def shifted(value, axis, steps):
    count = lax.axis_size(axis)
    return lax.ppermute(value, axis, [(i, (i + steps) % count) for i in range(count)])


def owner(block, info):
    return (info[0] + X - block % X) % X, (info[1] + block // X) % CORES


def first_tokens(block, kind, info):
    owner_x, owner_core = owner(block, info)
    if kind == 0:
        return ((info[2] * X + owner_x) * CORES + owner_core) * TOKENS, info[3]
    return ((owner_x % 2) * CORES + owner_core) * TOKENS, info[4 + info[2] * 2 + owner_x // 2]


def row_tokens():
    return lax.broadcasted_iota(jnp.int32, (1, ROWS), 1) // 8


def prompt_scores(block, kind, info, keys, queries):
    scores = lax.dot_general(keys, queries, NT, preferred_element_type=F32) * SCALE2
    key = lax.broadcasted_iota(jnp.int32, (keys.shape[0], 1), 0)
    key_pos = (key // TOKENS) * (BLOCKS * TOKENS) + key % TOKENS + (info[0] * CORES + info[1]) * TOKENS
    if kind == 1:
        limit = jnp.zeros((1, ROWS), jnp.int32) + (info[3] - 1)
    else:
        limit = first_tokens(block, 0, info)[0] + row_tokens()
    return jnp.where(key_pos <= limit, scores, MASKED)


def roll_scores(block, info, keys, queries):
    scores = lax.dot_general(keys, queries, NT, preferred_element_type=F32) * SCALE2
    key_pos = lax.broadcasted_iota(jnp.int32, (TOKENS, 1), 0) + ((info[0] % 2) * CORES + info[1]) * TOKENS
    return jnp.where(key_pos <= first_tokens(block, 1, info)[0] + row_tokens(), scores, MASKED)


def per_extent(info):
    def run(body):
        short = info[3] <= SHORT_KEYS * BLOCKS
        pl.when(short)(lambda: body(SHORT_KEYS))
        pl.when(jnp.logical_not(short))(lambda: body(KEYS))

    return run


def partial_stats(scores, weight_grad):
    top = jnp.max(scores, axis=0, keepdims=True)
    weights = jnp.exp2(scores - top)
    total = jnp.sum(weights, axis=0, keepdims=True)
    product = jnp.sum(weights * weight_grad, axis=0, keepdims=True)
    return top + jnp.log2(total), product / total


def merged(first, second):
    (log_a, delta_a), (log_b, delta_b) = first, second
    top = jnp.maximum(log_a, log_b)
    share_a, share_b = jnp.exp2(log_a - top), jnp.exp2(log_b - top)
    total = share_a + share_b
    return top + jnp.log2(total), (delta_a * share_a + delta_b * share_b) / total


def fetch(refs, rows_s, sems):
    for i, ref in enumerate(refs):
        pltpu.make_async_copy(ref, rows_s.at[i], sems.at[i]).start()


def arrive(i, refs, rows_s, sems):
    pltpu.make_async_copy(refs[0], rows_s.at[i], sems.at[i]).wait()


def sees_roll(block, info):
    return owner(block, info)[0] // 2 == info[0] // 2


def stats_kernel(info, *refs):
    rows, (kv_ref, rkv_ref, out_ref, all_ref, rows_s, stats_s, sems, out_sems) = refs[:BLOCKS], refs[BLOCKS:]
    fetch(rows, rows_s, sems)

    def keep(block):
        return pltpu.make_async_copy(rows_s.at[block], all_ref.at[block], out_sems.at[block])

    @pl.loop(0, BLOCKS)
    def _(block):
        arrive(block, rows, rows_s, sems)
        keep(block).start()
        owner_x, owner_core = owner(block, info)
        at = owner_x * CORES + owner_core

        def put(kind, stats):
            stats_s[at, 2 * kind : 2 * kind + 1, :] = stats[0]
            stats_s[at, 2 * kind + 1 : 2 * kind + 2, :] = stats[1]

        @per_extent(info)
        def _(extent):
            for kind in (0, 1):
                queries, grads = rows_s[block, kind], rows_s[block, 2 + kind]
                scores = prompt_scores(block, kind, info, kv_ref[:extent, :HD], queries)
                weight_grad = lax.dot_general(kv_ref[:extent, HD:], grads, NT, preferred_element_type=F32)
                put(kind, partial_stats(scores, weight_grad))

        @pl.when(sees_roll(block, info))
        def _():
            roll = roll_scores(block, info, rkv_ref[:, :HD], rows_s[block, 1])
            roll_grad = lax.dot_general(rkv_ref[:, HD:], rows_s[block, 3], NT, preferred_element_type=F32)
            put(1, merged((stats_s[at, 2:3, :], stats_s[at, 3:4, :]), partial_stats(roll, roll_grad)))

    for peer in range(BLOCKS):
        out_ref[peer] = stats_s[...]
    for block in range(BLOCKS):
        keep(block).wait()


def combined(stats_ref, block, kind, info):
    owner_x, owner_core = owner(block, info)
    at = owner_x * CORES + owner_core
    logs, deltas = stats_ref[:, at, 2 * kind, :], stats_ref[:, at, 2 * kind + 1, :]
    top = jnp.max(logs, axis=0, keepdims=True)
    shares = jnp.exp2(logs - top)
    total = jnp.sum(shares, axis=0, keepdims=True)
    start, length = first_tokens(block, kind, info)
    log_total = jnp.where(start + row_tokens() < length, top + jnp.log2(total), -MASKED)
    return log_total, jnp.sum(shares * deltas, axis=0, keepdims=True) / total


def block_grads(scores, weight_grad, log_total, delta, queries, grads, keys_t):
    weights = jnp.exp2(scores - log_total)
    score_grad = (weights * (weight_grad - delta)).astype(BF16)
    key_part = jnp.dot(score_grad, queries, preferred_element_type=F32)
    value_part = jnp.dot(weights.astype(BF16), grads, preferred_element_type=F32)
    query_t = jnp.dot(keys_t, score_grad, preferred_element_type=F32)
    return query_t, key_part, value_part


def grads_kernel(info, rows_ref, stats_ref, kv_ref, kt_ref, rkv_ref, rkt_ref, *refs):
    (dq0_ref, dq1_ref, dkv_ref, drk_ref, drv_ref, rows_s, dqt_s, acc, roll_acc, sems) = refs
    rows = [rows_ref.at[block] for block in range(BLOCKS)]
    fetch(rows, rows_s, sems)
    acc[...] = jnp.zeros_like(acc)
    roll_acc[...] = jnp.zeros_like(roll_acc)

    @pl.loop(0, BLOCKS)
    def _(block):
        arrive(block, rows, rows_s, sems)

        @per_extent(info)
        def _(extent):
            for kind in (0, 1):
                log_total, delta = combined(stats_ref, block, kind, info)
                queries, grads = rows_s[block, kind], rows_s[block, 2 + kind]
                scores = prompt_scores(block, kind, info, kv_ref[:extent, :HD], queries)
                weight_grad = lax.dot_general(kv_ref[:extent, HD:], grads, NT, preferred_element_type=F32)
                query_t, key_part, value_part = block_grads(
                    scores, weight_grad, log_total, delta, queries, grads, kt_ref[:, :extent]
                )
                dqt_s[kind] = query_t
                acc[:extent, :HD] += key_part
                acc[:extent, HD:] += value_part

        @pl.when(sees_roll(block, info))
        def _():
            log_total, delta = combined(stats_ref, block, 1, info)
            queries, grads = rows_s[block, 1], rows_s[block, 3]
            roll = roll_scores(block, info, rkv_ref[:, :HD], queries)
            roll_grad = lax.dot_general(rkv_ref[:, HD:], grads, NT, preferred_element_type=F32)
            query_r, key_r, value_r = block_grads(roll, roll_grad, log_total, delta, queries, grads, rkt_ref[...])
            dqt_s[1] += query_r
            roll_acc[:, :HD] += key_r
            roll_acc[:, HD:] += value_r

        for kind in (0, 1):
            out = (dqt_s[kind] * SCALING).T.astype(BF16)
            at = slice(kind * ROWS, kind * ROWS + ROWS)

            @pl.when(block < X)
            def _():
                dq0_ref[block, at, :] = out

            @pl.when(block >= X)
            def _():
                dq1_ref[block - X, at, :] = out

    dkv_ref[:, :HD] = (acc[:, :HD] * SCALING).astype(BF16)
    dkv_ref[:, HD:] = acc[:, HD:].astype(BF16)
    drk_ref[...] = (roll_acc[:, :HD] * SCALING).astype(BF16)
    drv_ref[...] = roll_acc[:, HD:].astype(BF16)


def finish_kernel(back_ref, dk_ref, dv_ref):
    total = jnp.sum(back_ref[...].astype(F32), axis=0)
    for head in range(total.shape[0]):
        dk_ref[:, head, :] = total[head, :, :HD].astype(BF16)
        dv_ref[:, head, :] = total[head, :, HD:].astype(BF16)


VMEM = pl.BlockSpec(memory_space=pltpu.VMEM)
SMEM = pl.BlockSpec(memory_space=pltpu.SMEM)
HBM = pl.BlockSpec(memory_space=pltpu.HBM)
PARAMS = pltpu.CompilerParams(vmem_limit_bytes=52 * 2**20)
COST = 2 * 1024 * 576 * HD


WAIT_FLOPS = 100 * 10**9


def cost(flops, byte_count):
    return pl.CostEstimate(flops=flops, bytes_accessed=byte_count, transcendentals=0)


def call_stats(info, rows, kv, rkv):
    return pl.pallas_call(
        stats_kernel,
        out_shape=(
            jax.ShapeDtypeStruct((BLOCKS, BLOCKS, 4, ROWS), F32),
            jax.ShapeDtypeStruct((BLOCKS, 4, ROWS, HD), BF16),
        ),
        in_specs=[SMEM] + [HBM] * BLOCKS + [VMEM] * 2,
        out_specs=(VMEM, HBM),
        scratch_shapes=[
            pltpu.VMEM((BLOCKS, 4, ROWS, HD), BF16),
            pltpu.VMEM((BLOCKS, 4, ROWS), F32),
            pltpu.SemaphoreType.DMA((BLOCKS,)),
            pltpu.SemaphoreType.DMA((BLOCKS,)),
        ],
        compiler_params=PARAMS,
        cost_estimate=cost(2 * 8 * COST, 5 * 2**20),
        name="row_stats",
    )(info, *rows, kv, rkv)


def call_grads(info, rows, stats, kv, kt, rkv, rkt):
    half = jax.ShapeDtypeStruct((X, 2 * ROWS, HD), BF16)
    roll = jax.ShapeDtypeStruct((TOKENS, HD), BF16)
    return pl.pallas_call(
        grads_kernel,
        out_shape=(half, half, jax.ShapeDtypeStruct((KEYS, 2 * HD), BF16), roll, roll),
        in_specs=[SMEM, HBM] + [VMEM] * 5,
        out_specs=(VMEM,) * 5,
        scratch_shapes=[
            pltpu.VMEM((BLOCKS, 4, ROWS, HD), BF16),
            pltpu.VMEM((2, HD, ROWS), F32),
            pltpu.VMEM((KEYS, 2 * HD), F32),
            pltpu.VMEM((TOKENS, 2 * HD), F32),
            pltpu.SemaphoreType.DMA((BLOCKS,)),
        ],
        compiler_params=PARAMS,
        cost_estimate=cost(5 * 8 * COST, 7 * 2**20),
        name="row_grads",
    )(info, rows, stats, kv, kt, rkv, rkt)


def call_finish(back):
    tokens, heads = back.shape[2], back.shape[1]
    out = jax.ShapeDtypeStruct((tokens, heads, HD), BF16)
    return pl.pallas_call(
        finish_kernel,
        out_shape=(out, out),
        in_specs=[VMEM],
        out_specs=(VMEM, VMEM),
        compiler_params=pltpu.CompilerParams(vmem_limit_bytes=4 * 2**20),
        cost_estimate=cost(WAIT_FLOPS, 2**18),
        name="sum_planes",
    )(back)


def per_device(q_prompt, k_prompt, v_prompt, grad_prompt, q_roll, k_roll, v_roll, grad_roll, prompt_len, roll_len):
    zl, x, core = (lax.axis_index(name) for name in CTX)
    pair = jnp.transpose(jnp.concatenate([k_prompt, v_prompt], axis=-1), (1, 0, 2))
    sent = jnp.broadcast_to(pair[None], (ZL,) + pair.shape).reshape(ZL * pair.shape[0], *pair.shape[1:])
    kv = lax.all_to_all(sent, FAR, split_axis=0, concat_axis=0, tiled=True).reshape(KEYS, 2 * HD)
    own = jnp.stack([q_prompt, q_roll, grad_prompt, grad_roll]).reshape(4, ROWS, HD)
    rows = [own] + [shifted(own, "x", steps) for steps in range(1, X)]
    rows = rows + [shifted(r, "core", 1) for r in rows]
    rkv = jnp.concatenate([k_roll, v_roll], axis=-1).reshape(TOKENS, 2 * HD)
    info = jnp.concatenate([jnp.stack([x, core, zl]).astype(jnp.int32), prompt_len, roll_len])
    stats, rows = call_stats(info, rows, kv, rkv)
    stats = lax.all_to_all(stats, NEAR, split_axis=0, concat_axis=0, tiled=True)
    dq_same, dq_other, dkv, drk, drv = call_grads(info, rows, stats, kv, kv[:, :HD].T, rkv, rkv[:, :HD].T)
    groups = k_prompt.shape[1]
    back = lax.all_to_all(
        dkv.reshape(ZL * groups, TOKENS // groups, 2 * HD), FAR, split_axis=0, concat_axis=0, tiled=True
    )
    arrived = shifted(dq_other, "core", 1)
    halves = (dq_same.astype(F32) + arrived.astype(F32)).astype(BF16)
    parts = [halves[0]] + [shifted(halves[steps], "x", -steps) for steps in range(1, X)]
    dq = [
        sum(part[first : first + ROWS].astype(F32) for part in parts).astype(BF16).reshape(q_prompt.shape)
        for first in (0, ROWS)
    ]
    back, *dq = lax.optimization_barrier((back, *dq))
    dk_prompt, dv_prompt = call_finish(back.reshape(ZL, groups, TOKENS // groups, 2 * HD))
    return (dq[0], dk_prompt, dv_prompt, dq[1], drk.reshape(k_roll.shape), drv.reshape(v_roll.shape))


def solution(mesh):
    names = tuple(name for name, _ in AXES)
    fine = Mesh(mesh.devices.reshape([size for _, size in AXES]), names)
    by_head, by_token = P(CTX, GRP, None), P(CTX + GRP, None, None)
    return jax.shard_map(
        per_device,
        mesh=fine,
        in_specs=(by_head, by_token, by_token, by_head, by_head, by_head, by_head, by_head, P(), P()),
        out_specs=(by_head, by_token, by_token, by_head, by_head, by_head),
        check_vma=False,
    )
```
